128 devices in a mesh: rep: 16 (over z_hi, x, core), tp: 8 (over z_lo, y).
Axes of the slice: x: 4, y: 4, z: 4 (z_hi: 2, z_lo: 2; z = z_hi * 2 + z_lo), core: 2. Of those that a mesh axis runs over, the one named last changes fastest.
Arguments:
- out_master: float32 [4096, 8192], P(None, ('rep', 'tp')), may hold values from -1 to 1
- out_base: bfloat16 [4096, 8192], P(None, ('rep', 'tp')), may hold values from -1 to 1
- out_held: bfloat16 [4096, 8192], P('tp'), may hold values from -1 to 1
- out_scales: int32 [32, 64], replicated, may hold values from -14 to -11, as said below
- query_master: float32 [8192, 4096], P(('rep', 'tp')), may hold values from -1 to 1
- query_base: bfloat16 [8192, 4096], P(('rep', 'tp')), may hold values from -1 to 1
- query_held: bfloat16 [8192, 4096], P(None, 'tp'), may hold values from -1 to 1
- query_scales: int32 [64, 32], replicated, may hold values from -14 to -11, as said below
- attention: bfloat16 [4, 2048, 4096], P(None, 'rep', 'tp'), may hold values from -6 to 6
- residual: bfloat16 [4, 2048, 8192], P(None, 'rep', 'tp'), may hold values from -100 to 100
- norm_gain: float32 [8192], P('tp'), may hold values from 0.25 to 1.75
Outputs:
- queries: bfloat16 [4, 2048, 4096], P(None, 'rep', 'tp')
The draws below stay inside these ranges and needn't reach their ends.
Inputs may be any that keep to these rules, and one draw needn't show every extreme that they name: `out_scales`: the exponent of the power-of-two scale of each 128 x 128 block. `query_scales`: the exponent of the power-of-two scale of each 128 x 128 block.
All inputs are finite; a program needn't handle non-finite values.
Results may differ from the reference program's by a relative error of at most 0.017.
Values may be sent and summed in bfloat16 or wider, within the bound.
No kernel may reach another device: no remote copies, remote signals or barrier semaphores. Data moves between devices by JAX's collectives and lax.ppermute only.
A program may use at most 128 MiB of HBM per device.

```python
import jax
import jax.numpy as jnp
from jax import lax

D = 8192
HW = 4096
BLOCK = 128
STEPS = 4
ROWS_ALL = 2048
N_TP = 8


def exact_power_drawn(exponents):
    shifted = jnp.left_shift(jnp.ones_like(exponents), exponents + 24)
    return shifted.astype(jnp.float32) * 2.0 ** (-24)


def projection_set(key, marker, height, width, fan_in):
    key = jax.random.fold_in(key, marker)
    subkeys = jax.random.split(key, 5)
    exponents = jax.random.randint(subkeys[0], (height // BLOCK, width // BLOCK), -14, -10, jnp.int32)
    clipped = jax.random.randint(subkeys[1], (height // BLOCK, width // BLOCK), 0, 16, jnp.int32) == 0
    amplitude = jnp.where(clipped, 0.6, 0.22)
    powers = jnp.repeat(jnp.repeat(exact_power_drawn(exponents) * amplitude, BLOCK, axis=0), BLOCK, axis=1)
    spread = jax.random.truncated_normal(subkeys[2], -4.5, 4.5, (height, width), jnp.float32)
    master = jax.random.truncated_normal(subkeys[3], -6.0, 6.0, (height, width), jnp.float32) * fan_in ** (-0.5)
    change = 448.0 * powers * spread
    previous = (master - change).astype(jnp.bfloat16)
    drift = 0.02 * fan_in ** (-0.5) * jax.random.truncated_normal(subkeys[4], -4.0, 4.0, (height, width), jnp.float32)
    holding = (previous.astype(jnp.float32) + drift).astype(jnp.bfloat16)
    return (exponents, master, previous, holding)


def out_set(key):
    return projection_set(key, 21, HW, D, HW)


def query_set(key):
    return projection_set(key, 22, D, HW, D)


def draw_out_scales(key, part):
    return projection_set(key, 21, HW, D, HW)[0]


def draw_out_master(key, part):
    return out_set(key)[1]


def draw_out_base(key, part):
    return out_set(key)[2]


def draw_out_held(key, part):
    return out_set(key)[3]


def draw_query_scales(key, part):
    return projection_set(key, 22, D, HW, D)[0]


def draw_query_master(key, part):
    return query_set(key)[1]


def draw_query_base(key, part):
    return query_set(key)[2]


def draw_query_held(key, part):
    return query_set(key)[3]


def draw_residual(key, part):
    key = jax.random.fold_in(key, 11)
    subkeys = jax.random.split(key, 3)
    columns = jnp.arange(D, dtype=jnp.float32) / (D - 1)
    values = jax.random.truncated_normal(subkeys[0], -6.0, 6.0, (STEPS, ROWS_ALL, D), jnp.float32)
    row_scale = jnp.exp(jax.random.uniform(subkeys[1], (STEPS, ROWS_ALL, 1), jnp.float32, jnp.log(0.3), jnp.log(3.0)))
    column_scale = 0.5 * jnp.exp(columns * jnp.log(3.0)) * jnp.exp(jax.random.uniform(subkeys[2], (D,), jnp.float32, jnp.log(0.55), jnp.log(1.8)))
    return (values * row_scale * column_scale[None, None, :]).astype(jnp.bfloat16)


def steps_of(key, extent, cuts, smallest, largest):
    factor_of, own = 1.0, jax.random.fold_in(key, 6)
    for axis_at, parts in cuts:
        heights = jnp.exp(jax.random.uniform(jax.random.fold_in(own, axis_at), (parts,), jnp.float32, smallest / len(cuts), largest / len(cuts)))
        factor_of = factor_of * jnp.repeat(heights, extent[axis_at] // parts).reshape([-1 if axis == axis_at else 1 for axis in range(len(extent))])
    return factor_of


def gaussian(rng, dims, scale, bound, cuts=(), kind=jnp.bfloat16):
    level = steps_of(rng, dims, cuts, -0.22, 0.18) if cuts else 1.0
    entries = jax.random.normal(rng, dims, jnp.float32) * scale * level
    return jnp.minimum(jnp.maximum(entries, -bound), bound).astype(kind)


def setup_inputs(seed: int = 0) -> dict:
    keys = jax.random.split(jax.random.key(seed), 12)
    return {
        "out_master": draw_out_master(jax.random.fold_in(keys[11], 71), 0),
        "out_base": draw_out_base(jax.random.fold_in(keys[11], 71), 0),
        "out_held": draw_out_held(jax.random.fold_in(keys[11], 71), 0),
        "out_scales": draw_out_scales(jax.random.fold_in(keys[11], 71), 0),
        "query_master": draw_query_master(jax.random.fold_in(keys[11], 71), 0),
        "query_base": draw_query_base(jax.random.fold_in(keys[11], 71), 0),
        "query_held": draw_query_held(jax.random.fold_in(keys[11], 71), 0),
        "query_scales": draw_query_scales(jax.random.fold_in(keys[11], 71), 0),
        "attention": gaussian(keys[8], (STEPS, ROWS_ALL, HW), 1.0, 6.0, ((1, 16), (2, 8))),
        "residual": draw_residual(jax.random.fold_in(keys[11], 71), 0),
        "norm_gain": jnp.clip(1.0 + 0.15 * jax.random.normal(keys[10], (D,), jnp.float32), 0.25, 1.75),
    }


def exact_power(exponents):
    shifted = jnp.left_shift(jnp.ones_like(exponents), exponents + 24)
    return shifted.astype(jnp.float32) * 2.0 ** (-24)

def block_powers(exponents):
    powers = exact_power(exponents)
    return jnp.repeat(jnp.repeat(powers, BLOCK, axis=0), BLOCK, axis=1)

def refresh(master, previous, holding, exponents):
    powers = block_powers(exponents)
    change = master.astype(jnp.float32) - previous.astype(jnp.float32)
    encoded = jnp.clip(change / powers, -448.0, 448.0).astype(jnp.bfloat16)
    encoded = lax.optimization_barrier(encoded)
    return (holding.astype(jnp.float32) + encoded.astype(jnp.float32) * powers).astype(jnp.bfloat16)

def reference(out_master, out_base, out_held, out_scales, query_master, query_base, query_held, query_scales, attention, residual, norm_gain):
    out_weight = refresh(out_master, out_base, out_held, out_scales)
    query_weight = refresh(query_master, query_base, query_held, query_scales)
    group_width = HW // N_TP
    results = []
    for decode_step in range(STEPS):
        mixture = jnp.zeros((ROWS_ALL, D), jnp.float32)
        for tp_rank in range(N_TP):
            lower = tp_rank * group_width
            product = jnp.dot(attention[decode_step, :, lower:lower + group_width], out_weight[lower:lower + group_width], preferred_element_type=jnp.float32)
            rounded = lax.optimization_barrier(product.astype(jnp.bfloat16))
            mixture = mixture + rounded.astype(jnp.float32)
        updated = residual[decode_step].astype(jnp.float32) + mixture
        inverse_rms = lax.rsqrt(lax.optimization_barrier(jnp.sum(updated * updated, axis=1)) / D + 1e-06)
        normed = (updated * inverse_rms[:, None] * norm_gain[None, :]).astype(jnp.bfloat16)
        results.append(jnp.dot(normed, query_weight, preferred_element_type=jnp.float32).astype(jnp.bfloat16))
    return jnp.stack(results)
```

```python
import jax
import jax.numpy as jnp
from jax import lax
from jax.sharding import PartitionSpec as P

BLOCK = 128
CHUNKS = 4
code_limit = 448.0
f32 = jnp.float32
bf16 = jnp.bfloat16


def exact_power(exponents):
    shifted = jnp.left_shift(jnp.ones_like(exponents), exponents + 24)
    return shifted.astype(f32) * 2.0 ** (-24)


def finish(master, base, held, exponents):
    powers = jnp.repeat(exact_power(exponents), BLOCK)[None, :]
    change = master - base.astype(f32)
    code = jnp.clip(change / powers, -code_limit, code_limit)
    code = lax.reduce_precision(code, 8, 7)
    return (held.astype(f32) + code * powers).astype(bf16)


def move_rep(v, dz=0, dx=0, dc=0):
    perm = []
    for r in range(16):
        z, x, c = r // 8, (r // 2) % 4, r % 2
        perm.append((r, (((z + dz) % 2) * 4 + (x + dx) % 4) * 2 + (c + dc) % 2))
    return lax.ppermute(v, "rep", perm)


def move_tp(v, dz=0, dy=0):
    perm = []
    for t in range(8):
        z, y = t // 4, t % 4
        perm.append((t, ((z + dz) % 2) * 4 + (y + dy) % 4))
    return lax.ppermute(v, "tp", perm)


def per_device(
    out_master,
    out_base,
    out_held,
    out_scales,
    query_master,
    query_base,
    query_held,
    query_scales,
    attention,
    residual,
    norm_gain,
):
    rep = lax.axis_index("rep")
    tp = lax.axis_index("tp")
    flat = rep * 8 + tp
    zh, xx, core = rep // 8, (rep // 2) % 4, rep % 2
    zl, yy = tp // 4, tp % 4
    width = out_held.shape[1]
    rows = attention.shape[0] * attention.shape[1]

    att = lax.all_gather(attention.reshape(rows, 512), "tp", axis=0, tiled=False)
    att = jnp.transpose(att, (1, 0, 2)).reshape(rows, 4096)

    out_slice = lax.dynamic_slice_in_dim(out_held, rep * 512, 512, 1)
    out_slice = jnp.transpose(out_slice.reshape(512, 8, 64), (1, 2, 0))
    out_slice = lax.all_to_all(out_slice, "tp", 0, 0, tiled=True)
    out_slice = jnp.transpose(out_slice, (1, 0, 2)).reshape(64, 4096)
    query_slice = lax.dynamic_slice_in_dim(query_held, rep * 512, 512, 0).reshape(8, 64, 512)
    query_slice = lax.all_to_all(query_slice, "tp", 0, 0, tiled=True)
    query_slice = jnp.transpose(query_slice, (1, 0, 2)).reshape(64, 4096)

    out_exp = lax.dynamic_index_in_dim(out_scales, flat // 2, 1, keepdims=False)
    query_exp = lax.dynamic_index_in_dim(query_scales, flat // 2, 0, keepdims=False)
    out_piece = finish(out_master.T, out_base.T, out_slice, out_exp)
    query_piece = finish(query_master, query_base, query_slice, query_exp)

    order = [
        ((zh + dz) % 2) * 4 + (xx + dx) % 4 for dx in (0, 3, 1, 2) for dz in (0, 1)
    ]
    res = residual.reshape(rows, 2, 8, 64)
    gain = norm_gain.reshape(1, 2, 8, 64)
    high = gain.astype(bf16)
    middle = (gain - high.astype(f32)).astype(bf16)
    low = (gain - high.astype(f32) - middle.astype(f32)).astype(bf16)
    res = jnp.concatenate([res, high, middle, low, jnp.zeros((13, 2, 8, 64), bf16)], axis=0)
    res = jnp.where(core == 0, res, res[:, ::-1])
    res = jnp.transpose(res, (2, 0, 1, 3)).reshape(8, rows + 16, 128)
    res = lax.all_to_all(res, "tp", 0, 0, tiled=True)
    res = jnp.stack([lax.dynamic_index_in_dim(res, i, 0, keepdims=False) for i in order])
    res = jnp.transpose(res.reshape(8, rows + 16, 2, 64), (1, 2, 0, 3)).reshape(rows + 16, 1024)
    gains = res[rows : rows + 3].astype(f32)
    gain = gains[0] + gains[1] + gains[2]
    res = res[:rows]

    own = out_piece
    partner = move_rep(own, dz=1)
    l_own = move_rep(own, dx=1)
    r_own = move_rep(own, dx=-1)
    f_own = move_rep(l_own, dx=1)
    l_par = move_rep(partner, dx=1)
    r_par = move_rep(partner, dx=-1)
    f_par = move_rep(r_par, dx=-1)
    mine = jnp.concatenate([own, partner, l_own, l_par, r_own, r_par, f_own, f_par], axis=0)
    other = move_rep(mine, dc=1)
    out_weight = jnp.concatenate([mine, other], axis=0)

    updated = (
        lax.dot_general(att, out_weight, (((1,), (1,)), ((), ())), preferred_element_type=f32)
        + res.astype(f32)
    )
    squares = jnp.sum(updated * updated, axis=1)
    squares = (
        squares + move_tp(squares, dy=1) + move_tp(squares, dy=-1) + move_tp(squares, dy=2)
    )
    squares = squares + move_tp(squares, dz=1)
    inverse = lax.rsqrt(squares / width + 1e-06)[:, None]
    hidden = (updated * gain[None, :]).astype(bf16)

    blocks = query_piece.reshape(64, 8, 512)
    blocks = jnp.stack(
        [
            lax.dynamic_index_in_dim(
                blocks, ((zl + dz) % 2) * 4 + (yy + dy) % 4, 1, keepdims=False
            )
            for dy in (2, 1, 3, 0)
            for dz in (0, 1)
        ],
        axis=0,
    )
    w = 512 // CHUNKS
    blocks = jnp.transpose(blocks.reshape(8, 64, CHUNKS, w), (2, 1, 0, 3)).reshape(
        CHUNKS, 64, 8 * w
    )
    partner = move_rep(blocks, dz=1)
    outs = []
    half = rows // 2
    for j in range(CHUNKS):
        own = jnp.concatenate([blocks[j], partner[j]], axis=0)
        left = move_rep(own, dx=1)
        right = move_rep(own, dx=-1)
        far_a = move_rep(left[:64], dx=1)
        far_b = move_rep(right[64:], dx=-1)
        mine = jnp.concatenate([own, left, right, far_a, far_b], axis=0)
        other = move_rep(mine, dc=1)
        weight = jnp.concatenate([mine, other], axis=0)
        partial = jnp.dot(hidden, weight, preferred_element_type=f32)
        far = partial[:, : 2 * w].astype(bf16)
        up = partial[:, 2 * w : 4 * w]
        down = partial[:, 4 * w : 6 * w]
        here = partial[:, 6 * w :]
        from_left = move_tp(far[:half], dy=1)
        from_right = move_tp(far[half:], dy=-1)
        up = jnp.concatenate([up[:half] + from_left.astype(f32), up[half:]], axis=0).astype(bf16)
        down = jnp.concatenate([down[:half], down[half:] + from_right.astype(f32)], axis=0).astype(
            bf16
        )
        here = here + move_tp(up, dy=1).astype(f32) + move_tp(down, dy=-1).astype(f32)
        across = move_tp(here[:, w:].astype(bf16), dz=1)
        outs.append(((here[:, :w] + across.astype(f32)) * inverse).astype(bf16))
    return jnp.concatenate(outs, axis=1).reshape(attention.shape[0], attention.shape[1], 512)


def solution(mesh):
    placed = (
        P(None, ("rep", "tp")),
        P(None, ("rep", "tp")),
        P("tp", None),
        P(),
        P(("rep", "tp"), None),
        P(("rep", "tp"), None),
        P(None, "tp"),
        P(),
        P(None, "rep", "tp"),
        P(None, "rep", "tp"),
        P("tp"),
    )
    return jax.shard_map(
        per_device, mesh=mesh, in_specs=placed, out_specs=P(None, "rep", "tp"), check_vma=False
    )
```

```python
import functools

import jax
import jax.numpy as jnp
from jax import lax
from jax.experimental import pallas as pl
from jax.experimental.pallas import tpu as pltpu
from jax.sharding import PartitionSpec as P

BLOCK = 128
CHUNKS = 2
code_limit = 448.0
f32 = jnp.float32
bf16 = jnp.bfloat16
NT = (((1,), (1,)), ((), ()))
ANY = pl.BlockSpec(memory_space=pl.ANY)
LIMIT = pltpu.CompilerParams(vmem_limit_bytes=48 * 2**20)


def move_rep(v, dz=0, dx=0, dc=0):
    perm = []
    for r in range(16):
        z, x, c = r // 8, (r // 2) % 4, r % 2
        perm.append((r, (((z + dz) % 2) * 4 + (x + dx) % 4) * 2 + (c + dc) % 2))
    return lax.ppermute(v, "rep", perm)


def move_tp(v, dz=0, dy=0):
    perm = []
    for t in range(8):
        z, y = t // 4, t % 4
        perm.append((t, ((z + dz) % 2) * 4 + (y + dy) % 4))
    return lax.ppermute(v, "tp", perm)


def relative(i, major, minor):
    k = i // 2
    shift = jnp.where(k == 0, 0, jnp.where(k == 1, 3, k - 1))
    return lax.rem(major + lax.rem(i, 2), 2) * 4 + lax.rem(minor + shift, 4)


def cost(mib, flops=0):
    return pl.CostEstimate(flops=flops, bytes_accessed=int(mib * 2**20), transcendentals=0)


def concat(pieces, gates=()):
    cols = pieces[0][0].shape[-1]
    grid = 2 if cols > 512 else 1
    wide = cols // grid
    counts, specs = [], []
    for a, at in pieces:
        if at is None:
            counts.append(a.shape[0])
            specs.append(pl.BlockSpec((a.shape[0], wide), lambda i: (0, i)))
        else:
            counts.append(a.shape[1])
            specs.append(
                pl.BlockSpec((1, a.shape[1], wide), functools.partial(lambda n, i: (n, 0, i), at))
            )
    total = sum(counts)

    def kernel(*refs):
        out = refs[-1]
        row = 0
        for ref, (_, at), count in zip(refs, pieces, counts):
            out[row : row + count, :] = ref[...] if at is None else ref[0]
            row += count

    return pl.pallas_call(
        kernel,
        out_shape=jax.ShapeDtypeStruct((total, cols), bf16),
        grid=(grid,),
        in_specs=specs + [ANY] * len(gates),
        out_specs=pl.BlockSpec((total, wide), lambda i: (0, i)),
        compiler_params=LIMIT,
        cost_estimate=cost(total * cols / 2**18),
    )(*[a for a, _ in pieces], *gates)


def pack_held(ids, out_held, query_held):
    def kernel(ids_ref, out_held_ref, query_held_ref, out_ref):
        turned = out_held_ref[...].astype(f32).T.astype(bf16)
        out_ref[:, :, :512] = turned.reshape(4, 64, 512)
        out_ref[:, :, 512:] = query_held_ref[...].reshape(4, 64, 512)

    return pl.pallas_call(
        kernel,
        out_shape=jax.ShapeDtypeStruct((8, 64, 1024), bf16),
        grid_spec=pltpu.PrefetchScalarGridSpec(
            num_scalar_prefetch=1,
            grid=(2,),
            in_specs=[
                pl.BlockSpec((512, 256), lambda i, ids: (0, ids[0] * 2 + i)),
                pl.BlockSpec((256, 512), lambda i, ids: (ids[0] * 2 + i, 0)),
            ],
            out_specs=pl.BlockSpec((4, 64, 1024), lambda i, ids: (i, 0, 0)),
        ),
        compiler_params=LIMIT,
        cost_estimate=cost(2),
    )(ids, out_held, query_held)


def refreshed(master, base, held, exponent):
    power = jnp.left_shift(jnp.int32(1), exponent + 24).astype(f32) * 2.0 ** (-24)
    inverse = jnp.left_shift(jnp.int32(1), -exponent).astype(f32)
    change = master - base.astype(f32)
    code = jnp.clip(change * inverse, -code_limit, code_limit).astype(bf16)
    return (held.astype(f32) + code.astype(f32) * power).astype(bf16)


def finish_out(ids, scales, master, base, held, gates):
    def kernel(ids_ref, scales_ref, master_ref, base_ref, held_ref, *rest):
        out_ref = rest[-1]
        column = (ids_ref[0] * 8 + ids_ref[1]) // 2
        for i in range(8):
            block = relative(jnp.int32(i), ids_ref[1] // 4, lax.rem(ids_ref[1], 4))
            for q in range(4):
                lanes = pl.ds(pl.multiple_of(block * 512 + q * 128, 128), 128)
                out_ref[:, i * 512 + q * 128 : i * 512 + q * 128 + 128] = refreshed(
                    master_ref[:, lanes],
                    base_ref[:, lanes],
                    held_ref[block, :, q * 128 : q * 128 + 128],
                    scales_ref[block * 4 + q, column],
                )

    return pl.pallas_call(
        kernel,
        out_shape=jax.ShapeDtypeStruct((64, 4096), bf16),
        grid_spec=pltpu.PrefetchScalarGridSpec(
            num_scalar_prefetch=2,
            grid=(1,),
            in_specs=[
                pl.BlockSpec((64, 4096), lambda i, ids, s: (0, 0)),
                pl.BlockSpec((64, 4096), lambda i, ids, s: (0, 0)),
                pl.BlockSpec((8, 64, 512), lambda i, ids, s: (0, 0, 0)),
            ]
            + [ANY] * len(gates),
            out_specs=pl.BlockSpec((64, 4096), lambda i, ids, s: (0, 0)),
        ),
        compiler_params=LIMIT,
        cost_estimate=cost(2.5),
    )(ids, scales, master, base, held, *gates)


def finish_query(ids, scales, master, base, held, gates):
    w = 512 // CHUNKS

    def kernel(ids_ref, scales_ref, master_ref, base_ref, held_ref, *rest):
        out_ref = rest[-1]
        row = (ids_ref[0] * 8 + ids_ref[1]) // 2
        for t in range(8):
            for q in range(4):
                lanes = slice(t * 512 + q * 128, t * 512 + q * 128 + 128)
                chunk, at = q * 128 // w, t * w + q * 128 % w
                out_ref[chunk, :, at : at + 128] = refreshed(
                    master_ref[:, lanes],
                    base_ref[:, lanes],
                    held_ref[t, :, q * 128 : q * 128 + 128],
                    scales_ref[row, t * 4 + q],
                )

    return pl.pallas_call(
        kernel,
        out_shape=jax.ShapeDtypeStruct((CHUNKS, 64, 8 * w), bf16),
        grid_spec=pltpu.PrefetchScalarGridSpec(
            num_scalar_prefetch=2,
            grid=(1,),
            in_specs=[
                pl.BlockSpec((64, 4096), lambda i, ids, s: (0, 0)),
                pl.BlockSpec((64, 4096), lambda i, ids, s: (0, 0)),
                pl.BlockSpec((8, 64, 512), lambda i, ids, s: (0, 0, 1)),
            ]
            + [ANY] * len(gates),
            out_specs=pl.BlockSpec((CHUNKS, 64, 8 * w), lambda i, ids, s: (0, 0, 0)),
        ),
        compiler_params=LIMIT,
        cost_estimate=cost(2.5),
    )(ids, scales, master, base, held, *gates)


def pack_residual(ids, residual, gain, gates):
    rows = residual.shape[0]

    def kernel(ids_ref, res_own, res_other, gain_own, gain_other, *rest):
        out_ref = rest[-1]
        at = lax.broadcasted_iota(jnp.int32, (16, 128), 0)
        for t in range(8):
            lanes = slice(t * 64, t * 64 + 64)
            out_ref[t, :rows, :] = jnp.concatenate(
                [res_own[:, lanes].astype(f32), res_other[:, lanes].astype(f32)], axis=1
            ).astype(bf16)
            value = jnp.concatenate([gain_own[:, lanes], gain_other[:, lanes]], axis=1)
            high = value.astype(bf16).astype(f32)
            middle = (value - high).astype(bf16).astype(f32)
            low = value - high - middle
            out_ref[t, rows:, :] = jnp.where(
                at == 0, high, jnp.where(at == 1, middle, jnp.where(at == 2, low, 0.0))
            ).astype(bf16)

    def own(i, ids):
        return (0, lax.rem(ids[0], 2))

    def other(i, ids):
        return (0, 1 - lax.rem(ids[0], 2))

    return pl.pallas_call(
        kernel,
        out_shape=jax.ShapeDtypeStruct((8, rows + 16, 128), bf16),
        grid_spec=pltpu.PrefetchScalarGridSpec(
            num_scalar_prefetch=1,
            grid=(1,),
            in_specs=[
                pl.BlockSpec((rows, 512), own),
                pl.BlockSpec((rows, 512), other),
                pl.BlockSpec((1, 512), own),
                pl.BlockSpec((1, 512), other),
            ]
            + [ANY] * len(gates),
            out_specs=pl.BlockSpec((8, rows + 16, 128), lambda i, ids: (0, 0, 0)),
        ),
        compiler_params=LIMIT,
        cost_estimate=cost(2),
    )(ids, residual, residual, gain, gain, *gates)


def out_product(ids, att, weights, packed):
    copies = [(n, i, g) for n, (_, groups) in enumerate(weights) for i, g in enumerate(groups)]
    rows = att[0].shape[0]

    def kernel(ids_ref, *refs):
        pieces, w_refs, packed_ref = refs[:8], refs[8 : 8 + len(weights)], refs[8 + len(weights)]
        hidden_ref, squares_ref, att_buf, w_buf, res_buf, sems = refs[-6:]
        waits = []
        for k in range(8):
            lanes = pl.ds(k * 512, 512)
            pair = [pltpu.make_async_copy(pieces[k], att_buf.at[k], sems.at[k, 0])]
            for m, (n, i, g) in enumerate(copies):
                pair.append(
                    pltpu.make_async_copy(
                        w_refs[n].at[pl.ds(i * 64, 64), lanes],
                        w_buf.at[k, pl.ds(g * 64, 64)],
                        sems.at[k, m + 1],
                    )
                )
            for copy in pair:
                copy.start()
            waits.append(pair)
        last = pltpu.make_async_copy(
            packed_ref, res_buf, sems.at[8, 0]
        )
        last.start()
        total = None
        for k in range(8):
            for copy in waits[k]:
                copy.wait()
            product = lax.dot_general(
                att_buf[k], w_buf[k], NT, preferred_element_type=f32
            )
            total = product if total is None else total + product
        last.wait()
        major, minor = ids_ref[0] // 8, lax.rem(ids_ref[0] // 2, 4)
        squares = jnp.zeros((rows, 128), f32)
        for part in range(2):
            lanes = slice(part * 64, part * 64 + 64)
            for g in range(0, 8, 2):
                residual, gain = [], []
                for d in range(2):
                    group = relative(jnp.int32(g + d), major, minor)
                    residual.append(res_buf[group, :rows, :].astype(f32)[:, lanes])
                    three = res_buf[group, rows:, :].astype(f32)[:, lanes]
                    gain.append(three[0:1] + three[1:2] + three[2:3])
                at = slice(part * 512 + g * 64, part * 512 + g * 64 + 128)
                updated = total[:, at] + jnp.concatenate(residual, axis=1)
                hidden_ref[:, at] = (updated * jnp.concatenate(gain, axis=1)).astype(bf16)
                squares = squares + updated * updated
        squares_ref[...] = squares

    return pl.pallas_call(
        kernel,
        out_shape=[
            jax.ShapeDtypeStruct((rows, 1024), bf16),
            jax.ShapeDtypeStruct((rows, 128), f32),
        ],
        grid_spec=pltpu.PrefetchScalarGridSpec(
            num_scalar_prefetch=1,
            grid=(1,),
            in_specs=[ANY] * (9 + len(weights)),
            out_specs=[
                pl.BlockSpec((rows, 1024), lambda i, ids: (0, 0)),
                pl.BlockSpec((rows, 128), lambda i, ids: (0, 0)),
            ],
            scratch_shapes=[
                pltpu.VMEM((8, rows, 512), bf16),
                pltpu.VMEM((8, 1024, 512), bf16),
                pltpu.VMEM((8, rows + 16, 128), bf16),
                pltpu.SemaphoreType.DMA((9, 17)),
            ],
        ),
        compiler_params=LIMIT,
        cost_estimate=cost(14, 2 * rows * 4096 * 1024),
    )(ids, *att, *[v for v, _ in weights], packed)


def query_product(hidden, weights, extra):
    rows = hidden.shape[0]
    cols = weights[0][0].shape[1]
    w = cols // 8
    tail = 0 if extra is None else 16

    def kernel(hidden_ref, *refs):
        w_refs, out_ref = refs[: len(weights)], refs[-5]
        h_buf, w_buf, out_buf, sems = refs[-4:]
        copies = [pltpu.make_async_copy(hidden_ref, h_buf, sems.at[0])]
        for n, (w_ref, (v, row)) in enumerate(zip(w_refs, weights)):
            copies.append(
                pltpu.make_async_copy(w_ref, w_buf.at[pl.ds(row, v.shape[0])], sems.at[n + 1])
            )
        for copy in copies:
            copy.start()
        if tail:
            for t in range(8):
                out_buf[t, rows:, :] = refs[len(weights)][...]
        for copy in copies:
            copy.wait()
        sends = []
        for t in range(8):
            out_buf[t, :rows, :] = jnp.dot(
                h_buf[...], w_buf[:, t * w : t * w + w], preferred_element_type=f32
            ).astype(bf16)
            copy = pltpu.make_async_copy(
                out_buf.at[t], out_ref.at[t], sems.at[1 + len(weights) + t]
            )
            copy.start()
            sends.append(copy)
        for copy in sends:
            copy.wait()

    return pl.pallas_call(
        kernel,
        out_shape=jax.ShapeDtypeStruct((8, rows + tail, w), bf16),
        in_specs=[ANY] * (1 + len(weights))
        + ([pl.BlockSpec(memory_space=pltpu.VMEM)] if tail else []),
        out_specs=ANY,
        scratch_shapes=[
            pltpu.VMEM((rows, 1024), bf16),
            pltpu.VMEM((1024, cols), bf16),
            pltpu.VMEM((8, rows + tail, w), bf16),
            pltpu.SemaphoreType.DMA((9 + len(weights),)),
        ],
        compiler_params=LIMIT,
        cost_estimate=cost(8, 2 * rows * 1024 * cols),
    )(hidden, *[v for v, _ in weights], *([extra] if tail else []))


def split3(value):
    high = value.astype(bf16)
    middle = (value - high.astype(f32)).astype(bf16)
    low = (value - high.astype(f32) - middle.astype(f32)).astype(bf16)
    return high, middle, low


def per_device(
    out_master,
    out_base,
    out_held,
    out_scales,
    query_master,
    query_base,
    query_held,
    query_scales,
    attention,
    residual,
    norm_gain,
):
    ids = jnp.stack([lax.axis_index("rep"), lax.axis_index("tp")]).astype(jnp.int32)
    width = out_held.shape[1]
    steps = attention.shape[0]
    rows = steps * attention.shape[1]
    w = 512 // CHUNKS

    held = pack_held(ids, out_held, query_held)
    a_own = concat([(attention.reshape(rows, 512), None)], (held,))
    held = lax.all_to_all(held, "tp", 0, 0, tiled=True)

    a_par = move_tp(a_own, dz=1)
    a_l_own = move_tp(a_own, dy=1)
    a_r_own = move_tp(a_own, dy=-1)
    a_f_own = move_tp(a_l_own, dy=1)
    a_l_par = move_tp(a_par, dy=1)
    a_r_par = move_tp(a_par, dy=-1)
    a_f_par = move_tp(a_r_par, dy=-1)
    att = [a_own, a_par, a_l_own, a_l_par, a_r_own, a_r_par, a_f_own, a_f_par]

    own = finish_out(
        ids, out_scales, out_master.T, out_base.T, held, (a_par, a_l_own, a_r_own)
    )
    par = move_rep(own, dz=1)
    l_own = move_rep(own, dx=1)
    r_own = move_rep(own, dx=-1)
    blocks = finish_query(ids, query_scales, query_master, query_base, held, (own,))
    blocks_par = move_rep(blocks, dz=1)
    packed = pack_residual(
        ids, residual.reshape(rows, 1024), norm_gain.reshape(1, 1024), (own,)
    )
    packed = lax.all_to_all(packed, "tp", 0, 0, tiled=True)

    f_own = move_rep(l_own, dx=1)
    l_par = move_rep(par, dx=1)
    r_par = move_rep(par, dx=-1)
    first = concat(
        [(v, None) for v in (own, par, l_own, r_own)], (a_f_own, a_l_par, a_r_par, blocks_par)
    )

    f_par = move_rep(r_par, dx=-1)
    second = concat([(v, None) for v in (l_par, r_par, f_own)], (a_f_par,))
    weights = [
        (own, (0,)),
        (par, (1,)),
        (l_own, (2,)),
        (l_par, (3,)),
        (r_own, (4,)),
        (r_par, (5,)),
        (f_own, (6,)),
        (f_par, (7,)),
        (move_rep(first, dc=1), (8, 9, 10, 12)),
        (move_rep(second, dc=1), (11, 13, 14)),
        (move_rep(f_par, dc=1), (15,)),
    ]

    hidden, squares = out_product(ids, att, weights, packed)
    squares = jnp.stack(split3(jnp.sum(squares, axis=1))).reshape(3 * rows // w, w)
    squares = jnp.concatenate([squares, jnp.zeros((16 - 3 * rows // w, w), bf16)], axis=0)

    sums = []
    gates = (l_par, r_par, f_own)
    before = hidden
    for j in range(CHUNKS):
        own = concat([(blocks, j), (blocks_par, j)], gates)
        left = move_rep(own, dx=1)
        right = move_rep(own, dx=-1)
        gates = (left, right)
        far_a = move_rep(left[:64], dx=1)
        far_b = move_rep(right[64:], dx=-1)
        near = concat([(v, None) for v in (own, left, right)], (before,))
        far = concat([(v, None) for v in (far_a, far_b)], (before,))
        weights = [
            (own, 0),
            (left, 128),
            (right, 256),
            (far_a, 384),
            (far_b, 448),
            (move_rep(near, dc=1), 512),
            (move_rep(far, dc=1), 896),
        ]
        partial = query_product(hidden, weights, squares if j == 0 else None)
        before = partial
        sums.append(lax.all_to_all(partial, "tp", 0, 0, tiled=True))
    squares = sums[0][:, rows:].astype(f32).reshape(8, -1)[:, : 3 * rows].reshape(8, 3, rows)
    inverse = lax.rsqrt(jnp.sum(squares, axis=(0, 1)) / width + 1e-06)[:, None]
    outs = [
        (jnp.sum(part[:, :rows].astype(f32), axis=0) * inverse).astype(bf16) for part in sums
    ]
    return jnp.concatenate(outs, axis=1).reshape(steps, rows // steps, 512)


def solution(mesh):
    placed = (
        P(None, ("rep", "tp")),
        P(None, ("rep", "tp")),
        P("tp", None),
        P(),
        P(("rep", "tp"), None),
        P(("rep", "tp"), None),
        P(None, "tp"),
        P(),
        P(None, "rep", "tp"),
        P(None, "rep", "tp"),
        P("tp"),
    )
    return jax.shard_map(
        per_device, mesh=mesh, in_specs=placed, out_specs=P(None, "rep", "tp"), check_vma=False
    )
```

```python
import functools

import jax
import jax.numpy as jnp
from jax import lax
from jax.experimental import pallas as pl
from jax.experimental.pallas import tpu as pltpu
from jax.sharding import PartitionSpec as P

BLOCK = 128
CHUNKS = 2
code_limit = 448.0
f32 = jnp.float32
bf16 = jnp.bfloat16
NT = (((1,), (1,)), ((), ()))
ANY = pl.BlockSpec(memory_space=pl.ANY)
LIMIT = pltpu.CompilerParams(vmem_limit_bytes=48 * 2**20)


def move_rep(v, dz=0, dx=0, dc=0):
    perm = []
    for r in range(16):
        z, x, c = r // 8, (r // 2) % 4, r % 2
        perm.append((r, (((z + dz) % 2) * 4 + (x + dx) % 4) * 2 + (c + dc) % 2))
    return lax.ppermute(v, "rep", perm)


def move_tp(v, dz=0, dy=0):
    perm = []
    for t in range(8):
        z, y = t // 4, t % 4
        perm.append((t, ((z + dz) % 2) * 4 + (y + dy) % 4))
    return lax.ppermute(v, "tp", perm)


def relative(i, major, minor):
    k = i // 2
    shift = jnp.where(k == 0, 0, jnp.where(k == 1, 3, k - 1))
    return lax.rem(major + lax.rem(i, 2), 2) * 4 + lax.rem(minor + shift, 4)


def cost(mib, flops=0):
    return pl.CostEstimate(flops=flops, bytes_accessed=int(mib * 2**20), transcendentals=0)


def concat(pieces, gates=()):
    cols = pieces[0][0].shape[-1]
    grid = 2 if cols > 512 else 1
    wide = cols // grid
    counts, specs = [], []
    for a, at in pieces:
        if at is None:
            counts.append(a.shape[0])
            specs.append(pl.BlockSpec((a.shape[0], wide), lambda i: (0, i)))
        else:
            counts.append(a.shape[1])
            specs.append(
                pl.BlockSpec((1, a.shape[1], wide), functools.partial(lambda n, i: (n, 0, i), at))
            )
    total = sum(counts)

    def kernel(*refs):
        out = refs[-1]
        row = 0
        for ref, (_, at), count in zip(refs, pieces, counts):
            out[row : row + count, :] = ref[...] if at is None else ref[0]
            row += count

    return pl.pallas_call(
        kernel,
        out_shape=jax.ShapeDtypeStruct((total, cols), bf16),
        grid=(grid,),
        in_specs=specs + [ANY] * len(gates),
        out_specs=pl.BlockSpec((total, wide), lambda i: (0, i)),
        compiler_params=LIMIT,
        cost_estimate=cost(total * cols / 2**18),
    )(*[a for a, _ in pieces], *gates)


def fence(values, gates=()):
    def kernel(*refs):
        pass

    return pl.pallas_call(
        kernel,
        out_shape=[jax.ShapeDtypeStruct(v.shape, v.dtype) for v in values],
        in_specs=[ANY] * (len(values) + len(gates)),
        out_specs=[ANY] * len(values),
        input_output_aliases={i: i for i in range(len(values))},
    )(*values, *gates)


def pack_held(ids, out_held, query_held):
    def kernel(ids_ref, out_held_ref, query_held_ref, out_ref):
        turned = out_held_ref[...].astype(f32).T.astype(bf16)
        out_ref[:, :, :512] = turned.reshape(4, 64, 512)
        out_ref[:, :, 512:] = query_held_ref[...].reshape(4, 64, 512)

    return pl.pallas_call(
        kernel,
        out_shape=jax.ShapeDtypeStruct((8, 64, 1024), bf16),
        grid_spec=pltpu.PrefetchScalarGridSpec(
            num_scalar_prefetch=1,
            grid=(2,),
            in_specs=[
                pl.BlockSpec((512, 256), lambda i, ids: (0, ids[0] * 2 + i)),
                pl.BlockSpec((256, 512), lambda i, ids: (ids[0] * 2 + i, 0)),
            ],
            out_specs=pl.BlockSpec((4, 64, 1024), lambda i, ids: (i, 0, 0)),
        ),
        compiler_params=LIMIT,
        cost_estimate=cost(2),
    )(ids, out_held, query_held)


def refreshed(master, base, held, exponent):
    power = jnp.left_shift(jnp.int32(1), exponent + 24).astype(f32) * 2.0 ** (-24)
    inverse = jnp.left_shift(jnp.int32(1), -exponent).astype(f32)
    change = master - base.astype(f32)
    code = jnp.clip(change * inverse, -code_limit, code_limit).astype(bf16)
    return (held.astype(f32) + code.astype(f32) * power).astype(bf16)


def finish_out(ids, scales, master, base, held, gates):
    def kernel(ids_ref, scales_ref, master_ref, base_ref, held_ref, *rest):
        out_ref = rest[-1]
        column = (ids_ref[0] * 8 + ids_ref[1]) // 2
        for i in range(8):
            block = relative(jnp.int32(i), ids_ref[1] // 4, lax.rem(ids_ref[1], 4))
            for q in range(4):
                lanes = pl.ds(pl.multiple_of(block * 512 + q * 128, 128), 128)
                out_ref[:, i * 512 + q * 128 : i * 512 + q * 128 + 128] = refreshed(
                    master_ref[:, lanes],
                    base_ref[:, lanes],
                    held_ref[block, :, q * 128 : q * 128 + 128],
                    scales_ref[block * 4 + q, column],
                )

    return pl.pallas_call(
        kernel,
        out_shape=jax.ShapeDtypeStruct((64, 4096), bf16),
        grid_spec=pltpu.PrefetchScalarGridSpec(
            num_scalar_prefetch=2,
            grid=(1,),
            in_specs=[
                pl.BlockSpec((64, 4096), lambda i, ids, s: (0, 0)),
                pl.BlockSpec((64, 4096), lambda i, ids, s: (0, 0)),
                pl.BlockSpec((8, 64, 512), lambda i, ids, s: (0, 0, 0)),
            ]
            + [ANY] * len(gates),
            out_specs=pl.BlockSpec((64, 4096), lambda i, ids, s: (0, 0)),
        ),
        compiler_params=LIMIT,
        cost_estimate=cost(2.5),
    )(ids, scales, master, base, held, *gates)


def finish_query(ids, scales, master, base, held, gates):
    w = 512 // CHUNKS

    def kernel(ids_ref, scales_ref, master_ref, base_ref, held_ref, *rest):
        out_ref = rest[-1]
        row = (ids_ref[0] * 8 + ids_ref[1]) // 2
        for t in range(8):
            for q in range(4):
                lanes = slice(t * 512 + q * 128, t * 512 + q * 128 + 128)
                chunk, at = q * 128 // w, t * w + q * 128 % w
                out_ref[chunk, :, at : at + 128] = refreshed(
                    master_ref[:, lanes],
                    base_ref[:, lanes],
                    held_ref[t, :, q * 128 : q * 128 + 128],
                    scales_ref[row, t * 4 + q],
                )

    return pl.pallas_call(
        kernel,
        out_shape=jax.ShapeDtypeStruct((CHUNKS, 64, 8 * w), bf16),
        grid_spec=pltpu.PrefetchScalarGridSpec(
            num_scalar_prefetch=2,
            grid=(1,),
            in_specs=[
                pl.BlockSpec((64, 4096), lambda i, ids, s: (0, 0)),
                pl.BlockSpec((64, 4096), lambda i, ids, s: (0, 0)),
                pl.BlockSpec((8, 64, 512), lambda i, ids, s: (0, 0, 1)),
            ]
            + [ANY] * len(gates),
            out_specs=pl.BlockSpec((CHUNKS, 64, 8 * w), lambda i, ids, s: (0, 0, 0)),
        ),
        compiler_params=LIMIT,
        cost_estimate=cost(2.5),
    )(ids, scales, master, base, held, *gates)


def pack_residual(ids, residual, gain, gates):
    rows = residual.shape[0]

    def kernel(ids_ref, res_own, res_other, gain_own, gain_other, *rest):
        out_ref = rest[-1]
        at = lax.broadcasted_iota(jnp.int32, (16, 128), 0)
        for t in range(8):
            lanes = slice(t * 64, t * 64 + 64)
            out_ref[t, :rows, :] = jnp.concatenate(
                [res_own[:, lanes].astype(f32), res_other[:, lanes].astype(f32)], axis=1
            ).astype(bf16)
            value = jnp.concatenate([gain_own[:, lanes], gain_other[:, lanes]], axis=1)
            high = value.astype(bf16).astype(f32)
            middle = (value - high).astype(bf16).astype(f32)
            low = value - high - middle
            out_ref[t, rows:, :] = jnp.where(
                at == 0, high, jnp.where(at == 1, middle, jnp.where(at == 2, low, 0.0))
            ).astype(bf16)

    def own(i, ids):
        return (0, lax.rem(ids[0], 2))

    def other(i, ids):
        return (0, 1 - lax.rem(ids[0], 2))

    return pl.pallas_call(
        kernel,
        out_shape=jax.ShapeDtypeStruct((8, rows + 16, 128), bf16),
        grid_spec=pltpu.PrefetchScalarGridSpec(
            num_scalar_prefetch=1,
            grid=(1,),
            in_specs=[
                pl.BlockSpec((rows, 512), own),
                pl.BlockSpec((rows, 512), other),
                pl.BlockSpec((1, 512), own),
                pl.BlockSpec((1, 512), other),
            ]
            + [ANY] * len(gates),
            out_specs=pl.BlockSpec((8, rows + 16, 128), lambda i, ids: (0, 0, 0)),
        ),
        compiler_params=LIMIT,
        cost_estimate=cost(2),
    )(ids, residual, residual, gain, gain, *gates)


def out_product(att, weights):
    copies = [(n, i, g) for n, (_, groups) in enumerate(weights) for i, g in enumerate(groups)]
    rows = att[0].shape[0]

    def kernel(*refs):
        pieces, w_refs = refs[:8], refs[8 : 8 + len(weights)]
        out_ref, att_buf, w_buf, sems = refs[-4:]
        waits = []
        for k in range(8):
            lanes = pl.ds(k * 512, 512)
            pair = [pltpu.make_async_copy(pieces[k], att_buf.at[k], sems.at[k, 0])]
            for m, (n, i, g) in enumerate(copies):
                pair.append(
                    pltpu.make_async_copy(
                        w_refs[n].at[pl.ds(i * 64, 64), lanes],
                        w_buf.at[k, pl.ds(g * 64, 64)],
                        sems.at[k, m + 1],
                    )
                )
            for copy in pair:
                copy.start()
            waits.append(pair)
        total = None
        for k in range(8):
            for copy in waits[k]:
                copy.wait()
            product = lax.dot_general(
                att_buf[k], w_buf[k], NT, preferred_element_type=f32
            )
            total = product if total is None else total + product
        out_ref[...] = total

    return pl.pallas_call(
        kernel,
        out_shape=jax.ShapeDtypeStruct((rows, 1024), f32),
        in_specs=[ANY] * (8 + len(weights)),
        out_specs=pl.BlockSpec(memory_space=pltpu.VMEM),
        scratch_shapes=[
            pltpu.VMEM((8, rows, 512), bf16),
            pltpu.VMEM((8, 1024, 512), bf16),
            pltpu.SemaphoreType.DMA((8, 17)),
        ],
        compiler_params=LIMIT,
        cost_estimate=cost(14, 2 * rows * 4096 * 1024),
    )(*att, *[v for v, _ in weights])


def add_residual(ids, mixture, packed):
    rows = mixture.shape[0]

    def kernel(ids_ref, mixture_ref, res_ref, hidden_ref, squares_ref):
        major, minor = ids_ref[0] // 8, lax.rem(ids_ref[0] // 2, 4)
        squares = jnp.zeros((rows, 128), f32)
        for part in range(2):
            lanes = slice(part * 64, part * 64 + 64)
            for g in range(0, 8, 2):
                residual, gain = [], []
                for d in range(2):
                    group = relative(jnp.int32(g + d), major, minor)
                    residual.append(res_ref[group, :rows, :].astype(f32)[:, lanes])
                    three = res_ref[group, rows:, :].astype(f32)[:, lanes]
                    gain.append(three[0:1] + three[1:2] + three[2:3])
                at = slice(part * 512 + g * 64, part * 512 + g * 64 + 128)
                updated = mixture_ref[:, at] + jnp.concatenate(residual, axis=1)
                hidden_ref[:, at] = (updated * jnp.concatenate(gain, axis=1)).astype(bf16)
                squares = squares + updated * updated
        squares_ref[...] = squares

    def whole(*shape):
        return pl.BlockSpec(shape, lambda i, ids: (0,) * len(shape))

    return pl.pallas_call(
        kernel,
        out_shape=[
            jax.ShapeDtypeStruct((rows, 1024), bf16),
            jax.ShapeDtypeStruct((rows, 128), f32),
        ],
        grid_spec=pltpu.PrefetchScalarGridSpec(
            num_scalar_prefetch=1,
            grid=(1,),
            in_specs=[whole(rows, 1024), whole(8, rows + 16, 128)],
            out_specs=[whole(rows, 1024), whole(rows, 128)],
        ),
        compiler_params=LIMIT,
        cost_estimate=cost(4),
    )(ids, mixture, packed)


def query_product(hidden, weights, extra):
    rows = hidden.shape[0]
    cols = weights[0][0].shape[1]
    w = cols // 8
    tail = 0 if extra is None else 16

    def kernel(hidden_ref, *refs):
        w_refs, out_ref = refs[: len(weights)], refs[-5]
        h_buf, w_buf, out_buf, sems = refs[-4:]
        copies = [pltpu.make_async_copy(hidden_ref, h_buf, sems.at[0])]
        for n, (w_ref, (v, row)) in enumerate(zip(w_refs, weights)):
            copies.append(
                pltpu.make_async_copy(w_ref, w_buf.at[pl.ds(row, v.shape[0])], sems.at[n + 1])
            )
        for copy in copies:
            copy.start()
        if tail:
            for t in range(8):
                out_buf[t, rows:, :] = refs[len(weights)][...]
        for copy in copies:
            copy.wait()
        sends = []
        for t in range(8):
            out_buf[t, :rows, :] = jnp.dot(
                h_buf[...], w_buf[:, t * w : t * w + w], preferred_element_type=f32
            ).astype(bf16)
            copy = pltpu.make_async_copy(
                out_buf.at[t], out_ref.at[t], sems.at[1 + len(weights) + t]
            )
            copy.start()
            sends.append(copy)
        for copy in sends:
            copy.wait()

    return pl.pallas_call(
        kernel,
        out_shape=jax.ShapeDtypeStruct((8, rows + tail, w), bf16),
        in_specs=[ANY] * (1 + len(weights))
        + ([pl.BlockSpec(memory_space=pltpu.VMEM)] if tail else []),
        out_specs=ANY,
        scratch_shapes=[
            pltpu.VMEM((rows, 1024), bf16),
            pltpu.VMEM((1024, cols), bf16),
            pltpu.VMEM((8, rows + tail, w), bf16),
            pltpu.SemaphoreType.DMA((9 + len(weights),)),
        ],
        compiler_params=LIMIT,
        cost_estimate=cost(8, 2 * rows * 1024 * cols),
    )(hidden, *[v for v, _ in weights], *([extra] if tail else []))


def split3(value):
    high = value.astype(bf16)
    middle = (value - high.astype(f32)).astype(bf16)
    low = (value - high.astype(f32) - middle.astype(f32)).astype(bf16)
    return high, middle, low


def per_device(
    out_master,
    out_base,
    out_held,
    out_scales,
    query_master,
    query_base,
    query_held,
    query_scales,
    attention,
    residual,
    norm_gain,
):
    ids = jnp.stack([lax.axis_index("rep"), lax.axis_index("tp")]).astype(jnp.int32)
    width = out_held.shape[1]
    steps = attention.shape[0]
    rows = steps * attention.shape[1]
    w = 512 // CHUNKS

    held = pack_held(ids, out_held, query_held)
    a_own = concat([(attention.reshape(rows, 512), None)], (held,))
    held = lax.all_to_all(held, "tp", 0, 0, tiled=True)

    a_par = move_tp(a_own, dz=1)
    a_l_own = move_tp(a_own, dy=1)
    a_r_own = move_tp(a_own, dy=-1)
    a_f_own = move_tp(a_l_own, dy=1)
    a_l_par = move_tp(a_par, dy=1)
    a_r_par = move_tp(a_par, dy=-1)
    a_f_par = move_tp(a_r_par, dy=-1)
    att = [a_own, a_par, a_l_own, a_l_par, a_r_own, a_r_par, a_f_own, a_f_par]

    own = finish_out(
        ids, out_scales, out_master.T, out_base.T, held, (a_par, a_l_own, a_r_own)
    )
    par = move_rep(own, dz=1)
    l_own = move_rep(own, dx=1)
    r_own = move_rep(own, dx=-1)
    blocks = finish_query(ids, query_scales, query_master, query_base, held, (own,))
    blocks_par = move_rep(blocks, dz=1)
    packed = pack_residual(
        ids, residual.reshape(rows, 1024), norm_gain.reshape(1, 1024), (own,)
    )
    packed = lax.all_to_all(packed, "tp", 0, 0, tiled=True)

    l_par = move_rep(par, dx=1)
    r_par = move_rep(par, dx=-1)
    l_own, r_par = fence((l_own, r_par), (l_par,))
    f_own = move_rep(l_own, dx=1)
    first = concat(
        [(v, None) for v in (own, par, l_own, r_own)], (a_f_own, a_l_par, a_r_par, blocks_par)
    )

    f_par = move_rep(r_par, dx=-1)
    second = concat([(v, None) for v in (l_par, r_par, f_own)], (a_f_par,))
    weights = [
        (own, (0,)),
        (par, (1,)),
        (l_own, (2,)),
        (l_par, (3,)),
        (r_own, (4,)),
        (r_par, (5,)),
        (f_own, (6,)),
        (f_par, (7,)),
        (move_rep(first, dc=1), (8, 9, 10, 12)),
        (move_rep(second, dc=1), (11, 13, 14)),
        (move_rep(f_par, dc=1), (15,)),
    ]

    hidden, squares = add_residual(ids, out_product(att, weights), packed)
    squares = jnp.stack(split3(jnp.sum(squares, axis=1))).reshape(3 * rows // w, w)
    squares = jnp.concatenate([squares, jnp.zeros((16 - 3 * rows // w, w), bf16)], axis=0)

    sums = []
    gates = (l_par, r_par, f_own)
    before = hidden
    for j in range(CHUNKS):
        own = concat([(blocks, j), (blocks_par, j)], gates)
        left = move_rep(own, dx=1)
        right = move_rep(own, dx=-1)
        gates = (left, right)
        far_a = move_rep(left[:64], dx=1)
        far_b = move_rep(right[64:], dx=-1)
        near = concat([(v, None) for v in (own, left, right)], (before,))
        far = concat([(v, None) for v in (far_a, far_b)], (before,))
        weights = [
            (own, 0),
            (left, 128),
            (right, 256),
            (far_a, 384),
            (far_b, 448),
            (move_rep(near, dc=1), 512),
            (move_rep(far, dc=1), 896),
        ]
        partial = query_product(hidden, weights, squares if j == 0 else None)
        before = partial
        sums.append(lax.all_to_all(partial, "tp", 0, 0, tiled=True))
    squares = sums[0][:, rows:].astype(f32).reshape(8, -1)[:, : 3 * rows].reshape(8, 3, rows)
    inverse = lax.rsqrt(jnp.sum(squares, axis=(0, 1)) / width + 1e-06)[:, None]
    outs = [
        (jnp.sum(part[:, :rows].astype(f32), axis=0) * inverse).astype(bf16) for part in sums
    ]
    return jnp.concatenate(outs, axis=1).reshape(steps, rows // steps, 512)


def solution(mesh):
    placed = (
        P(None, ("rep", "tp")),
        P(None, ("rep", "tp")),
        P("tp", None),
        P(),
        P(("rep", "tp"), None),
        P(("rep", "tp"), None),
        P(None, "tp"),
        P(),
        P(None, "rep", "tp"),
        P(None, "rep", "tp"),
        P("tp"),
    )
    return jax.shard_map(
        per_device, mesh=mesh, in_specs=placed, out_specs=P(None, "rep", "tp"), check_vma=False
    )
```

```python
import functools

import jax
import jax.numpy as jnp
from jax import lax
from jax.experimental import pallas as pl
from jax.experimental.pallas import tpu as pltpu
from jax.sharding import PartitionSpec as P

BLOCK = 128
CHUNKS = 2
code_limit = 448.0
f32 = jnp.float32
bf16 = jnp.bfloat16
NT = (((1,), (1,)), ((), ()))
ANY = pl.BlockSpec(memory_space=pl.ANY)
LIMIT = pltpu.CompilerParams(vmem_limit_bytes=48 * 2**20)


def move_rep(v, dz=0, dx=0, dc=0):
    perm = []
    for r in range(16):
        z, x, c = r // 8, (r // 2) % 4, r % 2
        perm.append((r, (((z + dz) % 2) * 4 + (x + dx) % 4) * 2 + (c + dc) % 2))
    return lax.ppermute(v, "rep", perm)


def move_tp(v, dz=0, dy=0):
    perm = []
    for t in range(8):
        z, y = t // 4, t % 4
        perm.append((t, ((z + dz) % 2) * 4 + (y + dy) % 4))
    return lax.ppermute(v, "tp", perm)


def relative(i, major, minor):
    k = i // 2
    shift = jnp.where(k == 0, 0, jnp.where(k == 1, 3, k - 1))
    return lax.rem(major + lax.rem(i, 2), 2) * 4 + lax.rem(minor + shift, 4)


def cost(mib, flops=0):
    return pl.CostEstimate(flops=flops, bytes_accessed=int(mib * 2**20), transcendentals=0)


def concat(pieces, gates=()):
    cols = pieces[0][0].shape[-1]
    counts = []
    for a, at in pieces:
        if isinstance(at, tuple):
            counts.append(at[1])
        else:
            counts.append(a.shape[0] if at is None else a.shape[1])
    total = sum(counts)

    def kernel(*refs):
        out, sems = refs[-2], refs[-1]
        row = 0
        copies = []
        for n, (ref, (_, at), count) in enumerate(zip(refs, pieces, counts)):
            if isinstance(at, tuple):
                ref = ref.at[pl.ds(at[0], count)]
            elif at is not None:
                ref = ref.at[at]
            copies.append(pltpu.make_async_copy(ref, out.at[pl.ds(row, count)], sems.at[n]))
            row += count
        load_all(copies)

    return pl.pallas_call(
        kernel,
        out_shape=jax.ShapeDtypeStruct((total, cols), bf16),
        in_specs=[ANY] * len(pieces) + [ANY] * len(gates),
        out_specs=pl.BlockSpec(memory_space=pltpu.VMEM),
        scratch_shapes=[pltpu.SemaphoreType.DMA((len(pieces),))],
        compiler_params=LIMIT,
        cost_estimate=cost(total * cols / 2**18),
    )(*[a for a, _ in pieces], *gates)


def load_all(copies):
    for copy in copies:
        copy.start()
    for copy in copies:
        copy.wait()


def fence(values, gates=()):
    def kernel(*refs):
        pass

    return pl.pallas_call(
        kernel,
        out_shape=[jax.ShapeDtypeStruct(v.shape, v.dtype) for v in values],
        in_specs=[ANY] * (len(values) + len(gates)),
        out_specs=[ANY] * len(values),
        input_output_aliases={i: i for i in range(len(values))},
    )(*values, *gates)


def pack_held(ids, out_held, query_held):
    def kernel(ids_ref, out_held_ref, query_held_ref, out_ref):
        turned = out_held_ref[...].astype(f32).T.astype(bf16)
        out_ref[:, :, :512] = turned.reshape(4, 64, 512)
        out_ref[:, :, 512:] = query_held_ref[...].reshape(4, 64, 512)

    return pl.pallas_call(
        kernel,
        out_shape=jax.ShapeDtypeStruct((8, 64, 1024), bf16),
        grid_spec=pltpu.PrefetchScalarGridSpec(
            num_scalar_prefetch=1,
            grid=(2,),
            in_specs=[
                pl.BlockSpec((512, 256), lambda i, ids: (0, ids[0] * 2 + i)),
                pl.BlockSpec((256, 512), lambda i, ids: (ids[0] * 2 + i, 0)),
            ],
            out_specs=pl.BlockSpec((4, 64, 1024), lambda i, ids: (i, 0, 0)),
        ),
        compiler_params=LIMIT,
        cost_estimate=cost(2),
    )(ids, out_held, query_held)


def refreshed(master, base, held, exponent):
    power = jnp.left_shift(jnp.int32(1), exponent + 24).astype(f32) * 2.0 ** (-24)
    inverse = jnp.left_shift(jnp.int32(1), -exponent).astype(f32)
    change = master - base.astype(f32)
    code = jnp.clip(change * inverse, -code_limit, code_limit).astype(bf16)
    return (held.astype(f32) + code.astype(f32) * power).astype(bf16)


def finish_out(ids, scales, master, base, held, gates):
    def kernel(ids_ref, scales_ref, master_ref, base_ref, held_ref, *rest):
        out_ref = rest[-1]
        column = (ids_ref[0] * 8 + ids_ref[1]) // 2
        for i in range(8):
            block = relative(jnp.int32(i), ids_ref[1] // 4, lax.rem(ids_ref[1], 4))
            for q in range(4):
                lanes = pl.ds(pl.multiple_of(block * 512 + q * 128, 128), 128)
                out_ref[:, i * 512 + q * 128 : i * 512 + q * 128 + 128] = refreshed(
                    master_ref[:, lanes],
                    base_ref[:, lanes],
                    held_ref[block, :, q * 128 : q * 128 + 128],
                    scales_ref[block * 4 + q, column],
                )

    return pl.pallas_call(
        kernel,
        out_shape=jax.ShapeDtypeStruct((64, 4096), bf16),
        grid_spec=pltpu.PrefetchScalarGridSpec(
            num_scalar_prefetch=2,
            grid=(1,),
            in_specs=[
                pl.BlockSpec((64, 4096), lambda i, ids, s: (0, 0)),
                pl.BlockSpec((64, 4096), lambda i, ids, s: (0, 0)),
                pl.BlockSpec((8, 64, 512), lambda i, ids, s: (0, 0, 0)),
            ]
            + [ANY] * len(gates),
            out_specs=pl.BlockSpec((64, 4096), lambda i, ids, s: (0, 0)),
        ),
        compiler_params=LIMIT,
        cost_estimate=cost(2.5),
    )(ids, scales, master, base, held, *gates)


def finish_query(ids, scales, master, base, held, gates):
    w = 512 // CHUNKS

    def kernel(ids_ref, scales_ref, master_ref, base_ref, held_ref, *rest):
        out_ref = rest[-1]
        row = (ids_ref[0] * 8 + ids_ref[1]) // 2
        for t in range(8):
            for q in range(4):
                lanes = slice(t * 512 + q * 128, t * 512 + q * 128 + 128)
                chunk, at = q * 128 // w, t * w + q * 128 % w
                out_ref[chunk, :, at : at + 128] = refreshed(
                    master_ref[:, lanes],
                    base_ref[:, lanes],
                    held_ref[t, :, q * 128 : q * 128 + 128],
                    scales_ref[row, t * 4 + q],
                )

    return pl.pallas_call(
        kernel,
        out_shape=jax.ShapeDtypeStruct((CHUNKS, 64, 8 * w), bf16),
        grid_spec=pltpu.PrefetchScalarGridSpec(
            num_scalar_prefetch=2,
            grid=(1,),
            in_specs=[
                pl.BlockSpec((64, 4096), lambda i, ids, s: (0, 0)),
                pl.BlockSpec((64, 4096), lambda i, ids, s: (0, 0)),
                pl.BlockSpec((8, 64, 512), lambda i, ids, s: (0, 0, 1)),
            ]
            + [ANY] * len(gates),
            out_specs=pl.BlockSpec((CHUNKS, 64, 8 * w), lambda i, ids, s: (0, 0, 0)),
        ),
        compiler_params=LIMIT,
        cost_estimate=cost(2.5),
    )(ids, scales, master, base, held, *gates)


def pack_residual(ids, residual, gain, gates):
    rows = residual.shape[0]

    def kernel(ids_ref, res_own, res_other, gain_own, gain_other, *rest):
        out_ref = rest[-1]
        at = lax.broadcasted_iota(jnp.int32, (16, 128), 0)
        for t in range(8):
            lanes = slice(t * 64, t * 64 + 64)
            out_ref[t, :rows, :] = jnp.concatenate(
                [res_own[:, lanes].astype(f32), res_other[:, lanes].astype(f32)], axis=1
            ).astype(bf16)
            value = jnp.concatenate([gain_own[:, lanes], gain_other[:, lanes]], axis=1)
            high = value.astype(bf16).astype(f32)
            middle = (value - high).astype(bf16).astype(f32)
            low = value - high - middle
            out_ref[t, rows:, :] = jnp.where(
                at == 0, high, jnp.where(at == 1, middle, jnp.where(at == 2, low, 0.0))
            ).astype(bf16)

    def own(i, ids):
        return (0, lax.rem(ids[0], 2))

    def other(i, ids):
        return (0, 1 - lax.rem(ids[0], 2))

    return pl.pallas_call(
        kernel,
        out_shape=jax.ShapeDtypeStruct((8, rows + 16, 128), bf16),
        grid_spec=pltpu.PrefetchScalarGridSpec(
            num_scalar_prefetch=1,
            grid=(1,),
            in_specs=[
                pl.BlockSpec((rows, 512), own),
                pl.BlockSpec((rows, 512), other),
                pl.BlockSpec((1, 512), own),
                pl.BlockSpec((1, 512), other),
            ]
            + [ANY] * len(gates),
            out_specs=pl.BlockSpec((8, rows + 16, 128), lambda i, ids: (0, 0, 0)),
        ),
        compiler_params=LIMIT,
        cost_estimate=cost(2),
    )(ids, residual, residual, gain, gain, *gates)


def out_product(att, weights):
    copies = [(n, i, g) for n, (_, groups) in enumerate(weights) for i, g in enumerate(groups)]
    rows = att[0].shape[0]

    def kernel(*refs):
        pieces, w_refs = refs[:8], refs[8 : 8 + len(weights)]
        out_ref, att_buf, w_buf, sems = refs[-4:]
        waits = []
        for k in range(8):
            lanes = pl.ds(k * 512, 512)
            pair = [pltpu.make_async_copy(pieces[k], att_buf.at[k], sems.at[k, 0])]
            for m, (n, i, g) in enumerate(copies):
                pair.append(
                    pltpu.make_async_copy(
                        w_refs[n].at[pl.ds(i * 64, 64), lanes],
                        w_buf.at[k, pl.ds(g * 64, 64)],
                        sems.at[k, m + 1],
                    )
                )
            for copy in pair:
                copy.start()
            waits.append(pair)
        total = None
        for k in range(8):
            for copy in waits[k]:
                copy.wait()
            product = lax.dot_general(
                att_buf[k], w_buf[k], NT, preferred_element_type=f32
            )
            total = product if total is None else total + product
        out_ref[...] = total

    return pl.pallas_call(
        kernel,
        out_shape=jax.ShapeDtypeStruct((rows, 1024), f32),
        in_specs=[ANY] * (8 + len(weights)),
        out_specs=pl.BlockSpec(memory_space=pltpu.VMEM),
        scratch_shapes=[
            pltpu.VMEM((8, rows, 512), bf16),
            pltpu.VMEM((8, 1024, 512), bf16),
            pltpu.SemaphoreType.DMA((8, 17)),
        ],
        compiler_params=LIMIT,
        cost_estimate=cost(14, 2 * rows * 4096 * 1024),
    )(*att, *[v for v, _ in weights])


def add_residual(ids, mixture, packed):
    rows = mixture.shape[0]

    def kernel(ids_ref, mixture_ref, res_ref, hidden_ref, squares_ref):
        major, minor = ids_ref[0] // 8, lax.rem(ids_ref[0] // 2, 4)
        squares = jnp.zeros((rows, 128), f32)
        for part in range(2):
            lanes = slice(part * 64, part * 64 + 64)
            for g in range(0, 8, 2):
                residual, gain = [], []
                for d in range(2):
                    group = relative(jnp.int32(g + d), major, minor)
                    residual.append(res_ref[group, :rows, :].astype(f32)[:, lanes])
                    three = res_ref[group, rows:, :].astype(f32)[:, lanes]
                    gain.append(three[0:1] + three[1:2] + three[2:3])
                at = slice(part * 512 + g * 64, part * 512 + g * 64 + 128)
                updated = mixture_ref[:, at] + jnp.concatenate(residual, axis=1)
                hidden_ref[:, at] = (updated * jnp.concatenate(gain, axis=1)).astype(bf16)
                squares = squares + updated * updated
        squares_ref[...] = squares

    def whole(*shape):
        return pl.BlockSpec(shape, lambda i, ids: (0,) * len(shape))

    return pl.pallas_call(
        kernel,
        out_shape=[
            jax.ShapeDtypeStruct((rows, 1024), bf16),
            jax.ShapeDtypeStruct((rows, 128), f32),
        ],
        grid_spec=pltpu.PrefetchScalarGridSpec(
            num_scalar_prefetch=1,
            grid=(1,),
            in_specs=[whole(rows, 1024), whole(8, rows + 16, 128)],
            out_specs=[whole(rows, 1024), whole(rows, 128)],
        ),
        compiler_params=LIMIT,
        cost_estimate=cost(4),
    )(ids, mixture, packed)


def query_product(hidden, weights, extra):
    rows = hidden.shape[0]
    cols = weights[0][0].shape[1]
    w = cols // 8
    tail = 0 if extra is None else 16

    def kernel(hidden_ref, *refs):
        w_refs, out_ref = refs[: len(weights)], refs[-5]
        h_buf, w_buf, out_buf, sems = refs[-4:]
        copies = [pltpu.make_async_copy(hidden_ref, h_buf, sems.at[0])]
        for n, (w_ref, (v, row)) in enumerate(zip(w_refs, weights)):
            copies.append(
                pltpu.make_async_copy(w_ref, w_buf.at[pl.ds(row, v.shape[0])], sems.at[n + 1])
            )
        for copy in copies:
            copy.start()
        if tail:
            for t in range(8):
                out_buf[t, rows:, :] = refs[len(weights)][...]
        for copy in copies:
            copy.wait()
        sends = []
        for t in range(8):
            out_buf[t, :rows, :] = jnp.dot(
                h_buf[...], w_buf[:, t * w : t * w + w], preferred_element_type=f32
            ).astype(bf16)
            copy = pltpu.make_async_copy(
                out_buf.at[t], out_ref.at[t], sems.at[1 + len(weights) + t]
            )
            copy.start()
            sends.append(copy)
        for copy in sends:
            copy.wait()

    return pl.pallas_call(
        kernel,
        out_shape=jax.ShapeDtypeStruct((8, rows + tail, w), bf16),
        in_specs=[ANY] * (1 + len(weights))
        + ([pl.BlockSpec(memory_space=pltpu.VMEM)] if tail else []),
        out_specs=ANY,
        scratch_shapes=[
            pltpu.VMEM((rows, 1024), bf16),
            pltpu.VMEM((1024, cols), bf16),
            pltpu.VMEM((8, rows + tail, w), bf16),
            pltpu.SemaphoreType.DMA((9 + len(weights),)),
        ],
        compiler_params=LIMIT,
        cost_estimate=cost(8, 2 * rows * 1024 * cols),
    )(hidden, *[v for v, _ in weights], *([extra] if tail else []))


def split3(value):
    high = value.astype(bf16)
    middle = (value - high.astype(f32)).astype(bf16)
    low = (value - high.astype(f32) - middle.astype(f32)).astype(bf16)
    return high, middle, low


def per_device(
    out_master,
    out_base,
    out_held,
    out_scales,
    query_master,
    query_base,
    query_held,
    query_scales,
    attention,
    residual,
    norm_gain,
):
    ids = jnp.stack([lax.axis_index("rep"), lax.axis_index("tp")]).astype(jnp.int32)
    width = out_held.shape[1]
    steps = attention.shape[0]
    rows = steps * attention.shape[1]
    w = 512 // CHUNKS

    held = pack_held(ids, out_held, query_held)
    a_own = concat([(attention.reshape(rows, 512), None)], (held,))
    held = lax.all_to_all(held, "tp", 0, 0, tiled=True)

    a_par = move_tp(a_own, dz=1)
    a_l_own = move_tp(a_own, dy=1)
    a_r_own = move_tp(a_own, dy=-1)
    a_f_own = move_tp(a_l_own, dy=1)
    a_l_par = move_tp(a_par, dy=1)
    a_r_par = move_tp(a_par, dy=-1)
    a_f_par = move_tp(a_r_par, dy=-1)
    att = [a_own, a_par, a_l_own, a_l_par, a_r_own, a_r_par, a_f_own, a_f_par]

    own = finish_out(
        ids, out_scales, out_master.T, out_base.T, held, (a_par, a_l_own, a_r_own)
    )
    par = move_rep(own, dz=1)
    l_own = move_rep(own, dx=1)
    r_own = move_rep(own, dx=-1)
    blocks = finish_query(ids, query_scales, query_master, query_base, held, (own,))
    blocks_par = move_rep(blocks, dz=1)
    packed = pack_residual(
        ids, residual.reshape(rows, 1024), norm_gain.reshape(1, 1024), (own,)
    )
    packed = lax.all_to_all(packed, "tp", 0, 0, tiled=True)

    l_par = move_rep(par, dx=1)
    r_par = move_rep(par, dx=-1)
    l_own, r_par = fence((l_own, r_par), (l_par,))
    f_own = move_rep(l_own, dx=1)
    first = concat(
        [(v, None) for v in (own, par, l_own, r_own)], (a_f_own, a_l_par, a_r_par, blocks_par)
    )

    f_par = move_rep(r_par, dx=-1)
    second = concat([(v, None) for v in (l_par, r_par, f_own)], (a_f_par,))
    weights = [
        (own, (0,)),
        (par, (1,)),
        (l_own, (2,)),
        (l_par, (3,)),
        (r_own, (4,)),
        (r_par, (5,)),
        (f_own, (6,)),
        (f_par, (7,)),
        (move_rep(first, dc=1), (8, 9, 10, 12)),
        (move_rep(second, dc=1), (11, 13, 14)),
        (move_rep(f_par, dc=1), (15,)),
    ]

    hidden, squares = add_residual(ids, out_product(att, weights), packed)
    squares = jnp.stack(split3(jnp.sum(squares, axis=1))).reshape(3 * rows // w, w)
    squares = jnp.concatenate([squares, jnp.zeros((16 - 3 * rows // w, w), bf16)], axis=0)

    sums = []
    gates = (l_par, r_par, f_own)
    before = hidden
    for j in range(CHUNKS):
        own = concat([(blocks, j), (blocks_par, j)], gates)
        left = move_rep(own, dx=1)
        right = move_rep(own, dx=-1)
        gates = (left, right)
        far_a = move_rep(concat([(left, (0, 64))]), dx=1)
        far_b = move_rep(concat([(right, (64, 64))]), dx=-1)
        near = concat([(v, None) for v in (own, left, right)], (before,))
        far = concat([(v, None) for v in (far_a, far_b)], (before,))
        weights = [
            (own, 0),
            (left, 128),
            (right, 256),
            (far_a, 384),
            (far_b, 448),
            (move_rep(near, dc=1), 512),
            (move_rep(far, dc=1), 896),
        ]
        partial = query_product(hidden, weights, squares if j == 0 else None)
        before = partial
        sums.append(lax.all_to_all(partial, "tp", 0, 0, tiled=True))
    squares = sums[0][:, rows:].astype(f32).reshape(8, -1)[:, : 3 * rows].reshape(8, 3, rows)
    inverse = lax.rsqrt(jnp.sum(squares, axis=(0, 1)) / width + 1e-06)[:, None]
    outs = [
        (jnp.sum(part[:, :rows].astype(f32), axis=0) * inverse).astype(bf16) for part in sums
    ]
    return jnp.concatenate(outs, axis=1).reshape(steps, rows // steps, 512)


def solution(mesh):
    placed = (
        P(None, ("rep", "tp")),
        P(None, ("rep", "tp")),
        P("tp", None),
        P(),
        P(("rep", "tp"), None),
        P(("rep", "tp"), None),
        P(None, "tp"),
        P(),
        P(None, "rep", "tp"),
        P(None, "rep", "tp"),
        P("tp"),
    )
    return jax.shard_map(
        per_device, mesh=mesh, in_specs=placed, out_specs=P(None, "rep", "tp"), check_vma=False
    )
```
